32 devices in a mesh: parts: 1, tm: 32 (over z, y, x, core).
Axes of the slice: x: 2, y: 2, z: 4, core: 2. Of those that a mesh axis runs over, the one named last changes fastest.
Arguments:
- traces: bfloat16 [64, 1151], P(('parts', 'tm')), may hold values from -6 to 6
- templates: bfloat16 [64, 64, 128], P('tm'), may hold values from -0.5 to 0.5
- station_of_slot: int32 [64], replicated, may hold values from 0 to 63, each once
- travel_offsets: int32 [64, 2], replicated, may hold values from 0 to 15
- stack_weights: bfloat16 [2, 128, 64], replicated, may hold values from -6 to 6
Outputs:
- peak_stack: float32 [64, 1024], P('parts', 'tm')
The draws below stay inside these ranges and needn't reach their ends.
Inputs may be any that keep to these rules, and one draw needn't show every extreme that they name: `station_of_slot`: each station stands in exactly one slot. `travel_offsets`: the greatest move-out is reached.
All inputs are finite; a program needn't handle non-finite values.
Results may differ from the reference program's by a relative error of at most 0.0011.
Values may be sent and summed in bfloat16 or wider, within the bound.
No kernel may reach another device: no remote copies, remote signals or barrier semaphores. Data moves between devices by JAX's collectives and lax.ppermute only.
A program may use at most 64 MiB of HBM per device.

```python
import jax
import jax.numpy as jnp
from jax import lax

STA_DEV = 2
K = 64
TL = 128
MAXOFF = 16
NB = 2
NPB = 128
S = 64
T_SIZE = 1024
DLEN = 1151
N_TM = 32


def plant(values, own_key, low, top_value):
    place = [jax.random.randint(jax.random.fold_in(own_key, axis), (), 0, length) for axis, length in enumerate(values.shape)]
    longest = values.shape.index(max(values.shape))
    beside = place[:longest] + [(place[longest] + 1) % values.shape[longest]] + place[longest + 1:]
    return values.at[tuple(place)].set(low).at[tuple(beside)].set(top_value)


def block_levels(rng, dims, shards, smallest, largest):
    loudness, own = 1.0, jax.random.fold_in(rng, 6)
    for dim, parts in shards:
        steps = jnp.exp(jax.random.uniform(jax.random.fold_in(own, dim), (parts,), jnp.float32, smallest / len(shards), largest / len(shards)))
        loudness = loudness * jnp.repeat(steps, dims[dim] // parts).reshape([-1 if axis == dim else 1 for axis in range(len(dims))])
    return loudness


def bell_draw(rng, shape, scale, limit, cuts=(), kind=jnp.bfloat16):
    result = jax.random.normal(rng, shape, jnp.float32) * scale
    if len(cuts) > 0:
        result = block_levels(rng, shape, cuts, -0.22, 0.18) * result
    return jnp.clip(result, min=-limit, max=limit).astype(kind)


def setup_inputs(seed: int = 0, part: int = 0) -> dict:
    splits = jax.random.split(jax.random.key(seed), 6)
    part_splits = jax.random.split(jax.random.fold_in(splits[5], part), 6)
    traces = bell_draw(part_splits[0], (S, DLEN), 1.0, 6.0, ((0, 32),))
    templates = bell_draw(splits[1], (S, K, TL), TL ** -0.5, 0.5, ((0, 32),))
    station_of_slot = jax.random.permutation(splits[2], S).astype(jnp.int32)
    travel_offsets = plant(jax.random.randint(splits[3], (S, NB), 0, MAXOFF), jax.random.fold_in(splits[3], 1), 0, MAXOFF - 1).astype(jnp.int32)
    stack_weights = bell_draw(splits[4], (NB, NPB, S), (S // 64) ** -0.5, 6.0)
    return dict(traces=traces, templates=templates, station_of_slot=station_of_slot, travel_offsets=travel_offsets, stack_weights=stack_weights)


def correlate(rows, waveforms):
    row_count = rows.shape[0]
    tmpl_count = waveforms.shape[1]
    tmpl_len = waveforms.shape[2]
    kernel = waveforms.reshape(row_count * tmpl_count, 1, tmpl_len)
    raw_corr = lax.conv_general_dilated(rows[None], kernel, (1,), 'VALID', dimension_numbers=('NCH', 'OIH', 'NCH'), feature_group_count=row_count, preferred_element_type=jnp.float32)[0]
    raw_corr = raw_corr.reshape(row_count, tmpl_count, -1)
    out_len = raw_corr.shape[2]
    squared = rows.astype(jnp.float32)
    squared = squared * squared
    running = jnp.cumsum(jnp.concatenate([jnp.zeros((row_count, 1), jnp.float32), squared], axis=1), axis=1)
    energy = (running[:, tmpl_len:tmpl_len + out_len] - running[:, :out_len]) / tmpl_len
    return (raw_corr / jnp.sqrt(tmpl_len * (energy[:, None, :] + 1e-05))).astype(jnp.bfloat16)

def reference(traces, templates, station_of_slot, travel_offsets, stack_weights):
    grouped = (traces.reshape(N_TM, STA_DEV, DLEN), templates.reshape(N_TM, STA_DEV, K, TL))
    ncc = lax.map(lambda pair: correlate(pair[0], pair[1]), grouped).reshape(S, K, T_SIZE)
    padded = jnp.pad(ncc, ((0, 0), (0, 0), (0, MAXOFF)))
    slot_weights = stack_weights[:, :, station_of_slot]
    slot_offsets = travel_offsets[station_of_slot]

    def one_block(block_id):
        shifted = jax.vmap(lambda row_trace, shift_by: lax.dynamic_slice_in_dim(row_trace, shift_by, T_SIZE, axis=1))(padded, slot_offsets[:, block_id])
        stacked = jnp.dot(slot_weights[block_id], shifted.reshape(S, K * T_SIZE), preferred_element_type=jnp.float32)
        return lax.optimization_barrier(jnp.max(stacked, axis=0))
    peaks = lax.map(one_block, jnp.arange(NB, dtype=jnp.int32))
    return lax.optimization_barrier(jnp.max(peaks, axis=0)).reshape(K, T_SIZE)
```

```python
import jax
import jax.numpy as jnp
from jax import lax
from jax.experimental import pallas as pl
from jax.experimental.pallas import tpu as pltpu
from jax.sharding import PartitionSpec as P

MAXOFF = 16
LANES = 128
F32 = jnp.float32
BF16 = jnp.bfloat16
BY_LANES = (((1,), (1,)), ((), ()))
BY_ROWS = (((0,), (0,)), ((), ()))


def on_diagonal(blocks):
    zero = jnp.zeros_like(blocks[0])
    return jnp.concatenate(
        [
            jnp.concatenate([b if i == j else zero for j in range(len(blocks))], axis=1)
            for i, b in enumerate(blocks)
        ],
        axis=0,
    )


def correlate_kernel(slab, traces_ref, templates_ref, out_ref, samples):
    row_count, length = traces_ref.shape
    tmpl_len = templates_ref.shape[2]
    groups = out_ref.shape[0]
    per_tile = LANES // slab
    samples[...] = jnp.zeros_like(samples)
    samples[:, :length] = traces_ref[...].astype(F32)
    waveforms = on_diagonal([templates_ref[s] for s in range(row_count)])
    ones = on_diagonal([jnp.ones(templates_ref.shape[1:], BF16)] * row_count)
    out_ref[groups - 1, :MAXOFF] = jnp.zeros((MAXOFF, out_ref.shape[2]), BF16)
    for tile in range(groups * slab // LANES):
        windows = []
        for s in range(row_count):
            stretch = samples[s : s + 1, tile * LANES : tile * LANES + LANES + tmpl_len]
            stretch = jnp.broadcast_to(stretch, (LANES, LANES + tmpl_len))
            rolled = pltpu.roll(stretch, tmpl_len + 1, 1, stride=1, stride_axis=0)
            windows.append(rolled[:, :tmpl_len])
        window = jnp.concatenate(windows, axis=1)
        square = window * window
        high = square.astype(BF16)
        low = (square - high.astype(F32)).astype(BF16)
        raw = lax.dot_general(window.astype(BF16), waveforms, BY_LANES, preferred_element_type=F32)
        power = lax.dot_general(high, ones, BY_LANES, preferred_element_type=F32)
        power += lax.dot_general(low, ones, BY_LANES, preferred_element_type=F32)
        ncc = (raw * lax.rsqrt(power + tmpl_len * 1e-05)).astype(BF16)
        for part in range(per_tile):
            d = tile * per_tile + part
            mine = ncc[LANES - (part + 1) * slab : LANES - part * slab]
            out_ref[d, MAXOFF:] = mine
            if d > 0:
                out_ref[d - 1, :MAXOFF] = mine[slab - MAXOFF :]


def weights_kernel(row_count, stations_ref, weights_ref, out_ref):
    slots = stations_ref.shape[1]
    first = lax.broadcasted_iota(jnp.int32, (slots, slots), 0)
    second = lax.broadcasted_iota(jnp.int32, (slots, slots), 1)
    groups = slots // row_count
    standing = (first == stations_ref[...]).astype(BF16)
    wanted = (first == (second % groups) * row_count + second // groups).astype(BF16)
    order = jnp.dot(standing, wanted, preferred_element_type=F32).astype(BF16)
    for b in range(weights_ref.shape[0]):
        out_ref[b] = lax.dot_general(
            weights_ref[b], order, BY_ROWS, preferred_element_type=F32
        ).astype(BF16)


def stack_kernel(
    slab, row_count, stations_ref, offsets_ref, weights_ref, parts_ref, out_ref, wide, moved
):
    groups, rows, lanes = parts_ref.shape
    blocks = weights_ref.shape[0]
    tmpl_count = lanes // row_count
    lane = lax.broadcasted_iota(jnp.int32, (slab, lanes), 1)

    def shift(src, unused):
        wide[...] = parts_ref[src].astype(F32)
        for b in range(blocks):
            moment = None
            for s in range(row_count):
                off = offsets_ref[b, stations_ref[src * row_count + s]]
                piece = wide[pl.ds(MAXOFF - off, slab), :]
                moment = piece if s == 0 else jnp.where(lane < s * tmpl_count, moment, piece)
            moved[b, pl.ds(src, slab, stride=groups), :] = moment
        return unused

    lax.fori_loop(0, groups, shift, 0, unroll=4)

    low_half = lax.broadcasted_iota(jnp.int32, (groups, lanes), 1) < tmpl_count
    times = 4
    for q in range(0, slab, times):
        best = None
        for b in range(blocks):
            columns = []
            for p in range(q, q + times, 2):
                even = moved[b, p * groups : (p + 1) * groups, :]
                odd = moved[b, (p + 1) * groups : (p + 2) * groups, :]
                top = jnp.where(low_half, even, pltpu.roll(odd, tmpl_count, 1))
                bottom = jnp.where(low_half, pltpu.roll(even, tmpl_count, 1), odd)
                columns.append(jnp.concatenate([top, bottom], axis=0).astype(BF16))
            stacked = jnp.dot(
                weights_ref[b], jnp.concatenate(columns, axis=1), preferred_element_type=F32
            )
            peak = jnp.max(stacked, axis=0, keepdims=True)
            best = peak if b == 0 else jnp.maximum(best, peak)
        for p in range(times):
            row = slab - 1 - q - p
            out_ref[row : row + 1, :] = best[:, p * tmpl_count : (p + 1) * tmpl_count]


def on_device(traces, templates, station_of_slot, travel_offsets, stack_weights):
    groups = lax.axis_size("tm")
    row_count, tmpl_count, tmpl_len = templates.shape
    slab = (traces.shape[1] - tmpl_len + 1) // groups
    slots = station_of_slot.shape[0]
    blocks, nodes, unused = stack_weights.shape
    lanes = row_count * tmpl_count
    vmem = pl.BlockSpec(memory_space=pltpu.VMEM)
    smem = pl.BlockSpec(memory_space=pltpu.SMEM)

    parts = pl.pallas_call(
        lambda *refs: correlate_kernel(slab, *refs),
        out_shape=jax.ShapeDtypeStruct((groups, slab + MAXOFF, lanes), BF16),
        in_specs=[vmem, vmem],
        out_specs=vmem,
        scratch_shapes=[pltpu.VMEM((row_count, groups * slab + LANES + tmpl_len), F32)],
        name="correlate",
    )(traces, templates)
    received = lax.all_to_all(parts, "tm", split_axis=0, concat_axis=0, tiled=True)
    weights = pl.pallas_call(
        lambda *refs: weights_kernel(row_count, *refs),
        out_shape=jax.ShapeDtypeStruct((blocks, nodes, slots), BF16),
        in_specs=[vmem, vmem],
        out_specs=vmem,
        name="order_weights",
    )(station_of_slot[None], jnp.swapaxes(stack_weights, 1, 2))
    peaks = pl.pallas_call(
        lambda *refs: stack_kernel(slab, row_count, *refs),
        out_shape=jax.ShapeDtypeStruct((slab, tmpl_count), F32),
        in_specs=[smem, smem, vmem, vmem],
        out_specs=vmem,
        scratch_shapes=[
            pltpu.VMEM((slab + MAXOFF, lanes), F32),
            pltpu.VMEM((blocks, slab * groups, lanes), F32),
        ],
        name="stack",
    )(station_of_slot, travel_offsets.T, weights, received)
    return peaks.T


def solution(mesh):
    return jax.shard_map(
        on_device,
        mesh=mesh,
        in_specs=(P(("parts", "tm"), None), P("tm", None, None), P(), P(), P()),
        out_specs=P("parts", "tm"),
        check_vma=False,
    )
```

```python
import jax
import jax.numpy as jnp
from jax import lax
from jax.experimental import pallas as pl
from jax.experimental.pallas import tpu as pltpu
from jax.sharding import PartitionSpec as P

MAXOFF = 16
LANES = 128
F32 = jnp.float32
BF16 = jnp.bfloat16
BY_LANES = (((1,), (1,)), ((), ()))
BY_ROWS = (((0,), (0,)), ((), ()))
PARAMS = pltpu.CompilerParams(vmem_limit_bytes=24 << 20)


def on_diagonal(blocks):
    zero = jnp.zeros_like(blocks[0])
    return jnp.concatenate(
        [
            jnp.concatenate([b if i == j else zero for j in range(len(blocks))], axis=1)
            for i, b in enumerate(blocks)
        ],
        axis=0,
    )


def slot_tables(row_count, stations_ref, offsets_ref, weights_ref, moves_ref, columns_ref):
    slots = stations_ref.shape[1]
    groups = slots // row_count
    first = lax.broadcasted_iota(jnp.int32, (slots, slots), 0)
    second = lax.broadcasted_iota(jnp.int32, (slots, slots), 1)
    standing = (first == stations_ref[...]).astype(BF16)
    wanted = (first == (second % groups) * row_count + second // groups).astype(BF16)
    order = jnp.dot(standing, wanted, preferred_element_type=F32).astype(BF16)
    moves = jnp.dot(offsets_ref[...].astype(BF16), order, preferred_element_type=F32)
    moves_ref[...] = moves.astype(jnp.int32)
    for b in range(weights_ref.shape[0]):
        columns = lax.dot_general(weights_ref[b], order, BY_ROWS, preferred_element_type=F32)
        columns_ref[b] = columns.astype(BF16)


def correlate_kernel(slab, *refs):
    sources, (out_ref, moves_ref, columns_ref) = refs[:5], refs[5:8]
    held, samples, sems = refs[8:13], refs[13], refs[14]
    copies = [pltpu.make_async_copy(a, b, sems.at[i]) for i, (a, b) in enumerate(zip(sources, held))]
    for copy in copies:
        copy.start()
    traces_ref, templates_ref = held[:2]
    row_count, length = traces_ref.shape
    tmpl_len = templates_ref.shape[2]
    groups = out_ref.shape[0]
    per_tile = LANES // slab
    samples[...] = jnp.zeros_like(samples)
    out_ref[groups - 1, :MAXOFF] = jnp.zeros((MAXOFF, out_ref.shape[2]), BF16)
    ones = on_diagonal([jnp.ones(templates_ref.shape[1:], BF16)] * row_count)
    for copy in copies:
        copy.wait()
    samples[:, :length] = traces_ref[...].astype(F32)
    waveforms = on_diagonal([templates_ref[s] for s in range(row_count)])
    for tile in range(groups * slab // LANES):
        windows = []
        for s in range(row_count):
            stretch = samples[s : s + 1, tile * LANES : tile * LANES + LANES + tmpl_len]
            stretch = jnp.broadcast_to(stretch, (LANES, LANES + tmpl_len))
            rolled = pltpu.roll(stretch, tmpl_len + 1, 1, stride=1, stride_axis=0)
            windows.append(rolled[:, :tmpl_len])
        window = jnp.concatenate(windows, axis=1)
        square = window * window
        high = square.astype(BF16)
        low = (square - high.astype(F32)).astype(BF16)
        raw = lax.dot_general(window.astype(BF16), waveforms, BY_LANES, preferred_element_type=F32)
        power = lax.dot_general(high, ones, BY_LANES, preferred_element_type=F32)
        power += lax.dot_general(low, ones, BY_LANES, preferred_element_type=F32)
        ncc = (raw * lax.rsqrt(power + tmpl_len * 1e-05)).astype(BF16)
        for part in range(per_tile):
            d = tile * per_tile + part
            mine = ncc[LANES - (part + 1) * slab : LANES - part * slab]
            out_ref[d, MAXOFF:] = mine
            if d > 0:
                out_ref[d - 1, :MAXOFF] = mine[slab - MAXOFF :]
    slot_tables(row_count, *held[2:], moves_ref, columns_ref)


def stack_kernel(slab, row_count, moves_ref, weights_ref, parts_ref, out_ref, wide, moved):
    groups, rows, lanes = parts_ref.shape
    blocks = weights_ref.shape[0]
    tmpl_count = lanes // row_count
    pitch = groups + 1
    lane = lax.broadcasted_iota(jnp.int32, (slab, lanes), 1)
    wide[...] = parts_ref[...].astype(F32)
    moves = moves_ref[...]
    for src in range(groups):
        for b in range(blocks):
            moment = None
            for s in range(row_count):
                start = MAXOFF - moves[b, s * groups + src]
                piece = wide[src, pl.ds(start, slab), :]
                moment = piece if s == 0 else jnp.where(lane < s * tmpl_count, moment, piece)
            moved[b, pl.ds(src, slab, stride=pitch), :] = moment

    low_half = lax.broadcasted_iota(jnp.int32, (groups, lanes), 1) < tmpl_count
    times = 4
    for q in range(0, slab, times):
        best = None
        for b in range(blocks):
            columns = []
            for p in range(q, q + times, 2):
                even = moved[b, p * pitch : p * pitch + groups, :]
                odd = moved[b, (p + 1) * pitch : (p + 1) * pitch + groups, :]
                top = jnp.where(low_half, even, pltpu.roll(odd, tmpl_count, 1))
                bottom = jnp.where(low_half, pltpu.roll(even, tmpl_count, 1), odd)
                columns.append(jnp.concatenate([top, bottom], axis=0).astype(BF16))
            stacked = jnp.dot(
                weights_ref[b], jnp.concatenate(columns, axis=1), preferred_element_type=F32
            )
            peak = jnp.max(stacked, axis=0, keepdims=True)
            best = peak if b == 0 else jnp.maximum(best, peak)
        for p in range(times):
            row = slab - 1 - q - p
            out_ref[row : row + 1, :] = best[:, p * tmpl_count : (p + 1) * tmpl_count]


def in_hbm(array):
    return pltpu.with_memory_space_constraint(array, pltpu.HBM)


def on_device(traces, templates, station_of_slot, travel_offsets, stack_weights):
    groups = lax.axis_size("tm")
    row_count, tmpl_count, tmpl_len = templates.shape
    slab = (traces.shape[1] - tmpl_len + 1) // groups
    slots = station_of_slot.shape[0]
    blocks, nodes, unused = stack_weights.shape
    lanes = row_count * tmpl_count
    vmem = pl.BlockSpec(memory_space=pltpu.VMEM)
    hbm = pl.BlockSpec(memory_space=pltpu.HBM)
    sources = (traces, templates, station_of_slot[None], travel_offsets.T, jnp.swapaxes(stack_weights, 1, 2))

    parts, moves, weights = pl.pallas_call(
        lambda *refs: correlate_kernel(slab, *refs),
        out_shape=(
            jax.ShapeDtypeStruct((groups, slab + MAXOFF, lanes), BF16),
            jax.ShapeDtypeStruct((blocks, slots), jnp.int32),
            jax.ShapeDtypeStruct((blocks, nodes, slots), BF16),
        ),
        in_specs=[hbm] * len(sources),
        out_specs=(vmem, vmem, vmem),
        scratch_shapes=[
            *(pltpu.VMEM(a.shape, a.dtype) for a in sources),
            pltpu.VMEM((row_count, groups * slab + LANES + tmpl_len), F32),
            pltpu.SemaphoreType.DMA((len(sources),)),
        ],
        compiler_params=PARAMS,
        name="correlate",
    )(*(in_hbm(a) for a in sources))
    received = lax.all_to_all(parts, "tm", split_axis=0, concat_axis=0, tiled=True)
    peaks = pl.pallas_call(
        lambda *refs: stack_kernel(slab, row_count, *refs),
        out_shape=jax.ShapeDtypeStruct((slab, tmpl_count), F32),
        in_specs=[vmem, vmem, vmem],
        out_specs=vmem,
        scratch_shapes=[
            pltpu.VMEM((groups, slab + MAXOFF, lanes), F32),
            pltpu.VMEM((blocks, slab * (groups + 1), lanes), F32),
        ],
        compiler_params=PARAMS,
        name="stack",
    )(moves, weights, received)
    return peaks.T


def solution(mesh):
    return jax.shard_map(
        on_device,
        mesh=mesh,
        in_specs=(P(("parts", "tm"), None), P("tm", None, None), P(), P(), P()),
        out_specs=P("parts", "tm"),
        check_vma=False,
    )
```

```python
import math

import jax
import jax.numpy as jnp
from jax import lax
from jax.experimental import pallas as pl
from jax.experimental.pallas import tpu as pltpu
from jax.sharding import PartitionSpec as P

MAXOFF = 16
LANES = 128
OUTER = 4
F32 = jnp.float32
BF16 = jnp.bfloat16
BY_LANES = (((1,), (1,)), ((), ()))
BY_ROWS = (((0,), (0,)), ((), ()))
PARAMS = pltpu.CompilerParams(vmem_limit_bytes=24 << 20)


def device_at(place, groups):
    outer = math.gcd(groups, OUTER)
    return (place % outer) * (groups // outer) + place // outer


def on_diagonal(blocks):
    zero = jnp.zeros_like(blocks[0])
    return jnp.concatenate(
        [
            jnp.concatenate([b if i == j else zero for j in range(len(blocks))], axis=1)
            for i, b in enumerate(blocks)
        ],
        axis=0,
    )


def slot_tables(row_count, stations_ref, offsets_ref, weights_ref, moves_ref, columns_ref):
    slots = stations_ref.shape[1]
    groups = slots // row_count
    first = lax.broadcasted_iota(jnp.int32, (slots, slots), 0)
    second = lax.broadcasted_iota(jnp.int32, (slots, slots), 1)
    standing = (first == stations_ref[...]).astype(BF16)
    wanted = (first == device_at(second % groups, groups) * row_count + second // groups).astype(BF16)
    order = jnp.dot(standing, wanted, preferred_element_type=F32).astype(BF16)
    moves = jnp.dot(offsets_ref[...].astype(BF16), order, preferred_element_type=F32)
    moves_ref[...] = moves.astype(jnp.int32)
    for b in range(weights_ref.shape[0]):
        columns = lax.dot_general(weights_ref[b], order, BY_ROWS, preferred_element_type=F32)
        columns_ref[b] = columns.astype(BF16)


def correlate_kernel(slab, *refs):
    sources, (out_ref, moves_ref, columns_ref) = refs[:5], refs[5:8]
    held, samples, sems = refs[8:13], refs[13], refs[14]
    copies = [pltpu.make_async_copy(a, b, sems.at[i]) for i, (a, b) in enumerate(zip(sources, held))]
    for copy in copies:
        copy.start()
    traces_ref, templates_ref = held[:2]
    row_count, length = traces_ref.shape
    tmpl_len = templates_ref.shape[2]
    groups = out_ref.shape[0]
    per_tile = LANES // slab
    places = [0] * groups
    for place in range(groups):
        places[device_at(place, groups)] = place
    samples[...] = jnp.zeros_like(samples)
    out_ref[places[groups - 1], :MAXOFF] = jnp.zeros((MAXOFF, out_ref.shape[2]), BF16)
    ones = on_diagonal([jnp.ones(templates_ref.shape[1:], BF16)] * row_count)
    for copy in copies:
        copy.wait()
    samples[:, :length] = traces_ref[...].astype(F32)
    waveforms = on_diagonal([templates_ref[s] for s in range(row_count)])
    slot_tables(row_count, *held[2:], moves_ref, columns_ref)
    for tile in range(groups * slab // LANES):
        windows = []
        for s in range(row_count):
            stretch = samples[s : s + 1, tile * LANES : tile * LANES + LANES + tmpl_len]
            stretch = jnp.broadcast_to(stretch, (LANES, LANES + tmpl_len))
            rolled = pltpu.roll(stretch, tmpl_len + 1, 1, stride=1, stride_axis=0)
            windows.append(rolled[:, :tmpl_len])
        window = jnp.concatenate(windows, axis=1)
        square = window * window
        high = square.astype(BF16)
        low = (square - high.astype(F32)).astype(BF16)
        raw = lax.dot_general(window.astype(BF16), waveforms, BY_LANES, preferred_element_type=F32)
        power = lax.dot_general(high, ones, BY_LANES, preferred_element_type=F32)
        power += lax.dot_general(low, ones, BY_LANES, preferred_element_type=F32)
        ncc = (raw * lax.rsqrt(power + tmpl_len * 1e-05)).astype(BF16)
        for part in range(per_tile):
            d = tile * per_tile + part
            mine = ncc[LANES - (part + 1) * slab : LANES - part * slab]
            out_ref[places[d], MAXOFF:] = mine
            if d > 0:
                out_ref[places[d - 1], :MAXOFF] = mine[slab - MAXOFF :]


def stack_kernel(slab, row_count, moves_ref, weights_ref, parts_ref, out_ref, wide, moved):
    groups, rows, lanes = parts_ref.shape
    blocks = weights_ref.shape[0]
    tmpl_count = lanes // row_count
    pitch = groups + 1
    lane = lax.broadcasted_iota(jnp.int32, (slab, lanes), 1)
    wide[...] = parts_ref[...].astype(F32)
    moves = moves_ref[...]
    for src in range(groups):
        for b in range(blocks):
            moment = None
            for s in range(row_count):
                start = MAXOFF - moves[b, s * groups + src]
                piece = wide[src, pl.ds(start, slab), :]
                moment = piece if s == 0 else jnp.where(lane < s * tmpl_count, moment, piece)
            moved[b, pl.ds(src, slab, stride=pitch), :] = moment

    low_half = lax.broadcasted_iota(jnp.int32, (groups, lanes), 1) < tmpl_count
    times = 4
    for q in range(0, slab, times):
        best = None
        for b in range(blocks):
            columns = []
            for p in range(q, q + times, 2):
                even = moved[b, p * pitch : p * pitch + groups, :]
                odd = moved[b, (p + 1) * pitch : (p + 1) * pitch + groups, :]
                top = jnp.where(low_half, even, pltpu.roll(odd, tmpl_count, 1))
                bottom = jnp.where(low_half, pltpu.roll(even, tmpl_count, 1), odd)
                columns.append(jnp.concatenate([top, bottom], axis=0).astype(BF16))
            stacked = jnp.dot(
                weights_ref[b], jnp.concatenate(columns, axis=1), preferred_element_type=F32
            )
            peak = jnp.max(stacked, axis=0, keepdims=True)
            best = peak if b == 0 else jnp.maximum(best, peak)
        for p in range(times):
            row = slab - 1 - q - p
            out_ref[row : row + 1, :] = best[:, p * tmpl_count : (p + 1) * tmpl_count]


def in_hbm(array):
    return pltpu.with_memory_space_constraint(array, pltpu.HBM)


def on_device(traces, templates, station_of_slot, travel_offsets, stack_weights):
    groups = lax.axis_size("tm")
    row_count, tmpl_count, tmpl_len = templates.shape
    slab = (traces.shape[1] - tmpl_len + 1) // groups
    slots = station_of_slot.shape[0]
    blocks, nodes, unused = stack_weights.shape
    lanes = row_count * tmpl_count
    vmem = pl.BlockSpec(memory_space=pltpu.VMEM)
    hbm = pl.BlockSpec(memory_space=pltpu.HBM)
    sources = (traces, templates, station_of_slot[None], travel_offsets.T, jnp.swapaxes(stack_weights, 1, 2))

    parts, moves, weights = pl.pallas_call(
        lambda *refs: correlate_kernel(slab, *refs),
        out_shape=(
            jax.ShapeDtypeStruct((groups, slab + MAXOFF, lanes), BF16),
            jax.ShapeDtypeStruct((blocks, slots), jnp.int32),
            jax.ShapeDtypeStruct((blocks, nodes, slots), BF16),
        ),
        in_specs=[hbm] * len(sources),
        out_specs=(vmem, vmem, vmem),
        scratch_shapes=[
            *(pltpu.VMEM(a.shape, a.dtype) for a in sources),
            pltpu.VMEM((row_count, groups * slab + LANES + tmpl_len), F32),
            pltpu.SemaphoreType.DMA((len(sources),)),
        ],
        compiler_params=PARAMS,
        name="correlate",
    )(*(in_hbm(a) for a in sources))
    order = [device_at(place, groups) for place in range(groups)]
    received = lax.all_to_all(
        parts, "tm", split_axis=0, concat_axis=0, axis_index_groups=[order], tiled=True
    )
    peaks = pl.pallas_call(
        lambda *refs: stack_kernel(slab, row_count, *refs),
        out_shape=jax.ShapeDtypeStruct((slab, tmpl_count), F32),
        in_specs=[vmem, vmem, vmem],
        out_specs=vmem,
        scratch_shapes=[
            pltpu.VMEM((groups, slab + MAXOFF, lanes), F32),
            pltpu.VMEM((blocks, slab * (groups + 1), lanes), F32),
        ],
        compiler_params=PARAMS,
        name="stack",
    )(moves, weights, received)
    return peaks.T


def solution(mesh):
    return jax.shard_map(
        on_device,
        mesh=mesh,
        in_specs=(P(("parts", "tm"), None), P("tm", None, None), P(), P(), P()),
        out_specs=P("parts", "tm"),
        check_vma=False,
    )
```

```python
import math

import jax
import jax.numpy as jnp
from jax import lax
from jax.experimental import pallas as pl
from jax.experimental.pallas import tpu as pltpu
from jax.sharding import PartitionSpec as P

MAXOFF = 16
LANES = 128
OUTER = 16
STRIDE = 5
F32 = jnp.float32
BF16 = jnp.bfloat16
BY_LANES = (((1,), (1,)), ((), ()))
BY_ROWS = (((0,), (0,)), ((), ()))
PARAMS = pltpu.CompilerParams(vmem_limit_bytes=24 << 20)


def device_at(place, groups):
    outer = math.gcd(groups, OUTER)
    place = place * (STRIDE if math.gcd(groups, STRIDE) == 1 else 1) % groups
    return (place % outer) * (groups // outer) + place // outer


def on_diagonal(blocks):
    zero = jnp.zeros_like(blocks[0])
    return jnp.concatenate(
        [
            jnp.concatenate([b if i == j else zero for j in range(len(blocks))], axis=1)
            for i, b in enumerate(blocks)
        ],
        axis=0,
    )


def slot_tables(row_count, stations_ref, offsets_ref, weights_ref, moves_ref, columns_ref):
    slots = stations_ref.shape[1]
    groups = slots // row_count
    first = lax.broadcasted_iota(jnp.int32, (slots, slots), 0)
    second = lax.broadcasted_iota(jnp.int32, (slots, slots), 1)
    standing = (first == stations_ref[...]).astype(BF16)
    wanted = (first == device_at(second % groups, groups) * row_count + second // groups).astype(BF16)
    order = jnp.dot(standing, wanted, preferred_element_type=F32).astype(BF16)
    moves = jnp.dot(offsets_ref[...].astype(BF16), order, preferred_element_type=F32)
    moves_ref[...] = moves.astype(jnp.int32)
    for b in range(weights_ref.shape[0]):
        columns = lax.dot_general(weights_ref[b], order, BY_ROWS, preferred_element_type=F32)
        columns_ref[b] = columns.astype(BF16)


def correlate_kernel(slab, *refs):
    sources, (out_ref, moves_ref, columns_ref) = refs[:5], refs[5:8]
    held, samples, sems = refs[8:13], refs[13], refs[14]
    copies = [pltpu.make_async_copy(a, b, sems.at[i]) for i, (a, b) in enumerate(zip(sources, held))]
    for copy in copies:
        copy.start()
    traces_ref, templates_ref = held[:2]
    row_count, length = traces_ref.shape
    tmpl_len = templates_ref.shape[2]
    groups = out_ref.shape[0]
    per_tile = LANES // slab
    places = [0] * groups
    for place in range(groups):
        places[device_at(place, groups)] = place
    samples[...] = jnp.zeros_like(samples)
    out_ref[places[groups - 1], :MAXOFF] = jnp.zeros((MAXOFF, out_ref.shape[2]), BF16)
    ones = on_diagonal([jnp.ones(templates_ref.shape[1:], BF16)] * row_count)
    for copy in copies:
        copy.wait()
    samples[:, :length] = traces_ref[...].astype(F32)
    waveforms = on_diagonal([templates_ref[s] for s in range(row_count)])
    slot_tables(row_count, *held[2:], moves_ref, columns_ref)
    for tile in range(groups * slab // LANES):
        windows = []
        for s in range(row_count):
            stretch = samples[s : s + 1, tile * LANES : tile * LANES + LANES + tmpl_len]
            stretch = jnp.broadcast_to(stretch, (LANES, LANES + tmpl_len))
            rolled = pltpu.roll(stretch, tmpl_len + 1, 1, stride=1, stride_axis=0)
            windows.append(rolled[:, :tmpl_len])
        window = jnp.concatenate(windows, axis=1)
        square = window * window
        high = square.astype(BF16)
        low = (square - high.astype(F32)).astype(BF16)
        raw = lax.dot_general(window.astype(BF16), waveforms, BY_LANES, preferred_element_type=F32)
        power = lax.dot_general(high, ones, BY_LANES, preferred_element_type=F32)
        power += lax.dot_general(low, ones, BY_LANES, preferred_element_type=F32)
        ncc = (raw * lax.rsqrt(power + tmpl_len * 1e-05)).astype(BF16)
        for part in range(per_tile):
            d = tile * per_tile + part
            mine = ncc[LANES - (part + 1) * slab : LANES - part * slab]
            out_ref[places[d], MAXOFF:] = mine
            if d > 0:
                out_ref[places[d - 1], :MAXOFF] = mine[slab - MAXOFF :]


def stack_kernel(slab, row_count, moves_ref, weights_ref, parts_ref, out_ref, wide, moved):
    groups, rows, lanes = parts_ref.shape
    blocks = weights_ref.shape[0]
    tmpl_count = lanes // row_count
    pitch = groups + 1
    lane = lax.broadcasted_iota(jnp.int32, (slab, lanes), 1)
    wide[...] = parts_ref[...].astype(F32)
    moves = moves_ref[...]
    for src in range(groups):
        for b in range(blocks):
            moment = None
            for s in range(row_count):
                start = MAXOFF - moves[b, s * groups + src]
                piece = wide[src, pl.ds(start, slab), :]
                moment = piece if s == 0 else jnp.where(lane < s * tmpl_count, moment, piece)
            moved[b, pl.ds(src, slab, stride=pitch), :] = moment

    low_half = lax.broadcasted_iota(jnp.int32, (groups, lanes), 1) < tmpl_count
    times = 4
    for q in range(0, slab, times):
        best = None
        for b in range(blocks):
            columns = []
            for p in range(q, q + times, 2):
                even = moved[b, p * pitch : p * pitch + groups, :]
                odd = moved[b, (p + 1) * pitch : (p + 1) * pitch + groups, :]
                top = jnp.where(low_half, even, pltpu.roll(odd, tmpl_count, 1))
                bottom = jnp.where(low_half, pltpu.roll(even, tmpl_count, 1), odd)
                columns.append(jnp.concatenate([top, bottom], axis=0).astype(BF16))
            stacked = jnp.dot(
                weights_ref[b], jnp.concatenate(columns, axis=1), preferred_element_type=F32
            )
            peak = jnp.max(stacked, axis=0, keepdims=True)
            best = peak if b == 0 else jnp.maximum(best, peak)
        for p in range(times):
            row = slab - 1 - q - p
            out_ref[row : row + 1, :] = best[:, p * tmpl_count : (p + 1) * tmpl_count]


def in_hbm(array):
    return pltpu.with_memory_space_constraint(array, pltpu.HBM)


def on_device(traces, templates, station_of_slot, travel_offsets, stack_weights):
    groups = lax.axis_size("tm")
    row_count, tmpl_count, tmpl_len = templates.shape
    slab = (traces.shape[1] - tmpl_len + 1) // groups
    slots = station_of_slot.shape[0]
    blocks, nodes, unused = stack_weights.shape
    lanes = row_count * tmpl_count
    vmem = pl.BlockSpec(memory_space=pltpu.VMEM)
    hbm = pl.BlockSpec(memory_space=pltpu.HBM)
    sources = (traces, templates, station_of_slot[None], travel_offsets.T, jnp.swapaxes(stack_weights, 1, 2))

    parts, moves, weights = pl.pallas_call(
        lambda *refs: correlate_kernel(slab, *refs),
        out_shape=(
            jax.ShapeDtypeStruct((groups, slab + MAXOFF, lanes), BF16),
            jax.ShapeDtypeStruct((blocks, slots), jnp.int32),
            jax.ShapeDtypeStruct((blocks, nodes, slots), BF16),
        ),
        in_specs=[hbm] * len(sources),
        out_specs=(vmem, vmem, vmem),
        scratch_shapes=[
            *(pltpu.VMEM(a.shape, a.dtype) for a in sources),
            pltpu.VMEM((row_count, groups * slab + LANES + tmpl_len), F32),
            pltpu.SemaphoreType.DMA((len(sources),)),
        ],
        compiler_params=PARAMS,
        name="correlate",
    )(*(in_hbm(a) for a in sources))
    order = [device_at(place, groups) for place in range(groups)]
    received = lax.all_to_all(
        parts, "tm", split_axis=0, concat_axis=0, axis_index_groups=[order], tiled=True
    )
    peaks = pl.pallas_call(
        lambda *refs: stack_kernel(slab, row_count, *refs),
        out_shape=jax.ShapeDtypeStruct((slab, tmpl_count), F32),
        in_specs=[vmem, vmem, vmem],
        out_specs=vmem,
        scratch_shapes=[
            pltpu.VMEM((groups, slab + MAXOFF, lanes), F32),
            pltpu.VMEM((blocks, slab * (groups + 1), lanes), F32),
        ],
        compiler_params=PARAMS,
        name="stack",
    )(moves, weights, received)
    return peaks.T


def solution(mesh):
    return jax.shard_map(
        on_device,
        mesh=mesh,
        in_specs=(P(("parts", "tm"), None), P("tm", None, None), P(), P(), P()),
        out_specs=P("parts", "tm"),
        check_vma=False,
    )
```

```python
import math

import jax
import jax.numpy as jnp
from jax import lax
from jax.experimental import pallas as pl
from jax.experimental.pallas import tpu as pltpu
from jax.sharding import PartitionSpec as P

MAXOFF = 16
LANES = 128
OUTER = 16
STRIDE = 5
F32 = jnp.float32
BF16 = jnp.bfloat16
BY_LANES = (((1,), (1,)), ((), ()))
BY_ROWS = (((0,), (0,)), ((), ()))
PARAMS = pltpu.CompilerParams(vmem_limit_bytes=24 << 20)


def device_at(place, groups):
    outer = math.gcd(groups, OUTER)
    place = place * (STRIDE if math.gcd(groups, STRIDE) == 1 else 1) % groups
    return (place % outer) * (groups // outer) + place // outer


def on_diagonal(blocks):
    zero = jnp.zeros_like(blocks[0])
    return jnp.concatenate(
        [
            jnp.concatenate([b if i == j else zero for j in range(len(blocks))], axis=1)
            for i, b in enumerate(blocks)
        ],
        axis=0,
    )


def slot_tables(row_count, stations_ref, offsets_ref, weights_ref, moves_ref, columns_ref):
    slots = stations_ref.shape[1]
    groups = slots // row_count
    first = lax.broadcasted_iota(jnp.int32, (slots, slots), 0)
    second = lax.broadcasted_iota(jnp.int32, (1, slots), 1)
    standing = (first == stations_ref[...]).astype(BF16)
    wanted = (first == device_at(second % groups, groups) * row_count + second // groups).astype(BF16)
    order = jnp.dot(standing, wanted, preferred_element_type=F32).astype(BF16)
    moves = jnp.dot(offsets_ref[...].astype(BF16), order, preferred_element_type=F32)
    moves_ref[...] = moves.astype(jnp.int32)
    for b in range(weights_ref.shape[0]):
        columns = lax.dot_general(weights_ref[b], order, BY_ROWS, preferred_element_type=F32)
        columns_ref[b] = columns.astype(BF16)


def correlate_kernel(slab, *refs):
    sources, (out_ref, moves_ref, columns_ref) = refs[:5], refs[5:8]
    held, samples, sems = refs[8:13], refs[13], refs[14]
    copies = [pltpu.make_async_copy(a, b, sems.at[i]) for i, (a, b) in enumerate(zip(sources, held))]
    for copy in copies:
        copy.start()
    traces_ref, templates_ref = held[:2]
    row_count, length = traces_ref.shape
    tmpl_len = templates_ref.shape[2]
    groups = out_ref.shape[0]
    per_tile = LANES // slab
    places = [0] * groups
    for place in range(groups):
        places[device_at(place, groups)] = place
    samples[...] = jnp.zeros_like(samples)
    out_ref[places[groups - 1], :MAXOFF] = jnp.zeros((MAXOFF, out_ref.shape[2]), BF16)
    ones = on_diagonal([jnp.ones(templates_ref.shape[1:], BF16)] * row_count)
    for copy in copies:
        copy.wait()
    samples[:, :length] = traces_ref[...].astype(F32)
    waveforms = on_diagonal([templates_ref[s] for s in range(row_count)])
    slot_tables(row_count, *held[2:], moves_ref, columns_ref)
    row = lax.broadcasted_iota(jnp.int32, (LANES, LANES), 0)
    lane = lax.broadcasted_iota(jnp.int32, (LANES, LANES), 1)

    def turned(s, tile):
        stretch = samples[s : s + 1, tile * LANES : (tile + 1) * LANES]
        return pltpu.roll(jnp.broadcast_to(stretch, (LANES, LANES)), 1, 1, stride=1, stride_axis=0)

    following = [turned(s, 0) for s in range(row_count)]
    for tile in range(groups * slab // LANES):
        present, following = following, [turned(s, tile + 1) for s in range(row_count)]
        windows = [jnp.where(lane <= row, a, b) for a, b in zip(present, following)]
        window = jnp.concatenate(windows, axis=1)
        square = window * window
        high = square.astype(BF16)
        low = (square - high.astype(F32)).astype(BF16)
        raw = lax.dot_general(window.astype(BF16), waveforms, BY_LANES, preferred_element_type=F32)
        power = lax.dot_general(high, ones, BY_LANES, preferred_element_type=F32)
        power += lax.dot_general(low, ones, BY_LANES, preferred_element_type=F32)
        ncc = (raw * lax.rsqrt(power + tmpl_len * 1e-05)).astype(BF16)
        for part in range(per_tile):
            d = tile * per_tile + part
            mine = ncc[LANES - (part + 1) * slab : LANES - part * slab]
            out_ref[places[d], MAXOFF:] = mine
            if d > 0:
                out_ref[places[d - 1], :MAXOFF] = mine[slab - MAXOFF :]


def stack_kernel(slab, row_count, moves_ref, weights_ref, parts_ref, out_ref, wide, moved):
    groups, rows, lanes = parts_ref.shape
    blocks = weights_ref.shape[0]
    tmpl_count = lanes // row_count
    pitch = groups + 1
    lane = lax.broadcasted_iota(jnp.int32, (slab, lanes), 1)
    wide[...] = parts_ref[...].astype(F32)
    moves = moves_ref[...]
    for src in range(groups):
        for b in range(blocks):
            moment = None
            for s in range(row_count):
                start = MAXOFF - moves[b, s * groups + src]
                piece = wide[src, pl.ds(start, slab), :]
                moment = piece if s == 0 else jnp.where(lane < s * tmpl_count, moment, piece)
            moved[b, pl.ds(src, slab, stride=pitch), :] = moment

    low_half = lax.broadcasted_iota(jnp.int32, (groups, lanes), 1) < tmpl_count
    times = 4
    for q in range(0, slab, times):
        best = None
        for b in range(blocks):
            columns = []
            for p in range(q, q + times, 2):
                even = moved[b, p * pitch : p * pitch + groups, :]
                odd = moved[b, (p + 1) * pitch : (p + 1) * pitch + groups, :]
                top = jnp.where(low_half, even, pltpu.roll(odd, tmpl_count, 1))
                bottom = jnp.where(low_half, pltpu.roll(even, tmpl_count, 1), odd)
                columns.append(jnp.concatenate([top, bottom], axis=0).astype(BF16))
            stacked = jnp.dot(
                weights_ref[b], jnp.concatenate(columns, axis=1), preferred_element_type=F32
            )
            peak = jnp.max(stacked, axis=0, keepdims=True)
            best = peak if b == 0 else jnp.maximum(best, peak)
        for p in range(times):
            row = slab - 1 - q - p
            out_ref[row : row + 1, :] = best[:, p * tmpl_count : (p + 1) * tmpl_count]


def in_hbm(array):
    return pltpu.with_memory_space_constraint(array, pltpu.HBM)


def on_device(traces, templates, station_of_slot, travel_offsets, stack_weights):
    groups = lax.axis_size("tm")
    row_count, tmpl_count, tmpl_len = templates.shape
    slab = (traces.shape[1] - tmpl_len + 1) // groups
    slots = station_of_slot.shape[0]
    blocks, nodes, unused = stack_weights.shape
    lanes = row_count * tmpl_count
    vmem = pl.BlockSpec(memory_space=pltpu.VMEM)
    hbm = pl.BlockSpec(memory_space=pltpu.HBM)
    sources = (traces, templates, station_of_slot[None], travel_offsets.T, jnp.swapaxes(stack_weights, 1, 2))

    parts, moves, weights = pl.pallas_call(
        lambda *refs: correlate_kernel(slab, *refs),
        out_shape=(
            jax.ShapeDtypeStruct((groups, slab + MAXOFF, lanes), BF16),
            jax.ShapeDtypeStruct((blocks, slots), jnp.int32),
            jax.ShapeDtypeStruct((blocks, nodes, slots), BF16),
        ),
        in_specs=[hbm] * len(sources),
        out_specs=(vmem, vmem, vmem),
        scratch_shapes=[
            *(pltpu.VMEM(a.shape, a.dtype) for a in sources),
            pltpu.VMEM((row_count, groups * slab + LANES + tmpl_len), F32),
            pltpu.SemaphoreType.DMA((len(sources),)),
        ],
        compiler_params=PARAMS,
        name="correlate",
    )(*(in_hbm(a) for a in sources))
    order = [device_at(place, groups) for place in range(groups)]
    received = lax.all_to_all(
        parts, "tm", split_axis=0, concat_axis=0, axis_index_groups=[order], tiled=True
    )
    peaks = pl.pallas_call(
        lambda *refs: stack_kernel(slab, row_count, *refs),
        out_shape=jax.ShapeDtypeStruct((slab, tmpl_count), F32),
        in_specs=[vmem, vmem, vmem],
        out_specs=vmem,
        scratch_shapes=[
            pltpu.VMEM((groups, slab + MAXOFF, lanes), F32),
            pltpu.VMEM((blocks, slab * (groups + 1), lanes), F32),
        ],
        compiler_params=PARAMS,
        name="stack",
    )(moves, weights, received)
    return peaks.T


def solution(mesh):
    return jax.shard_map(
        on_device,
        mesh=mesh,
        in_specs=(P(("parts", "tm"), None), P("tm", None, None), P(), P(), P()),
        out_specs=P("parts", "tm"),
        check_vma=False,
    )
```

```python
import math

import jax
import jax.numpy as jnp
from jax import lax
from jax.experimental import pallas as pl
from jax.experimental.pallas import tpu as pltpu
from jax.sharding import PartitionSpec as P

MAXOFF = 16
LANES = 128
OUTER = 16
STRIDE = 5
F32 = jnp.float32
BF16 = jnp.bfloat16
BY_LANES = (((1,), (1,)), ((), ()))
BY_ROWS = (((0,), (0,)), ((), ()))
PARAMS = pltpu.CompilerParams(vmem_limit_bytes=24 << 20)


def device_at(place, groups):
    outer = math.gcd(groups, OUTER)
    place = place * (STRIDE if math.gcd(groups, STRIDE) == 1 else 1) % groups
    device = (place % outer) * (groups // outer) + place // outer
    return device + 1 - 2 * (device % 2) if groups % 2 == 0 else device


def on_diagonal(blocks):
    zero = jnp.zeros_like(blocks[0])
    return jnp.concatenate(
        [
            jnp.concatenate([b if i == j else zero for j in range(len(blocks))], axis=1)
            for i, b in enumerate(blocks)
        ],
        axis=0,
    )


def slot_tables(row_count, stations_ref, offsets_ref, weights_ref, moves_ref, columns_ref):
    slots = stations_ref.shape[1]
    groups = slots // row_count
    first = lax.broadcasted_iota(jnp.int32, (slots, slots), 0)
    second = lax.broadcasted_iota(jnp.int32, (1, slots), 1)
    standing = (first == stations_ref[...]).astype(BF16)
    wanted = (first == device_at(second % groups, groups) * row_count + second // groups).astype(BF16)
    order = jnp.dot(standing, wanted, preferred_element_type=F32).astype(BF16)
    moves = jnp.dot(offsets_ref[...].astype(BF16), order, preferred_element_type=F32)
    moves_ref[...] = moves.astype(jnp.int32)
    for b in range(weights_ref.shape[0]):
        columns = lax.dot_general(weights_ref[b], order, BY_ROWS, preferred_element_type=F32)
        columns_ref[b] = columns.astype(BF16)


def correlate_kernel(slab, *refs):
    sources, (out_ref, moves_ref, columns_ref) = refs[:5], refs[5:8]
    held, samples, sems = refs[8:13], refs[13], refs[14]
    copies = [pltpu.make_async_copy(a, b, sems.at[i]) for i, (a, b) in enumerate(zip(sources, held))]
    for copy in copies:
        copy.start()
    traces_ref, templates_ref = held[:2]
    row_count, length = traces_ref.shape
    tmpl_len = templates_ref.shape[2]
    groups = out_ref.shape[0]
    per_tile = LANES // slab
    places = [0] * groups
    for place in range(groups):
        places[device_at(place, groups)] = place
    samples[...] = jnp.zeros_like(samples)
    out_ref[places[groups - 1], :MAXOFF] = jnp.zeros((MAXOFF, out_ref.shape[2]), BF16)
    ones = on_diagonal([jnp.ones(templates_ref.shape[1:], BF16)] * row_count)
    for copy in copies:
        copy.wait()
    samples[:, :length] = traces_ref[...].astype(F32)
    waveforms = on_diagonal([templates_ref[s] for s in range(row_count)])
    slot_tables(row_count, *held[2:], moves_ref, columns_ref)
    row = lax.broadcasted_iota(jnp.int32, (LANES, LANES), 0)
    lane = lax.broadcasted_iota(jnp.int32, (LANES, LANES), 1)

    def turned(s, tile):
        stretch = samples[s : s + 1, tile * LANES : (tile + 1) * LANES]
        return pltpu.roll(jnp.broadcast_to(stretch, (LANES, LANES)), 1, 1, stride=1, stride_axis=0)

    following = [turned(s, 0) for s in range(row_count)]
    for tile in range(groups * slab // LANES):
        present, following = following, [turned(s, tile + 1) for s in range(row_count)]
        windows = [jnp.where(lane <= row, a, b) for a, b in zip(present, following)]
        window = jnp.concatenate(windows, axis=1)
        square = window * window
        high = square.astype(BF16)
        low = (square - high.astype(F32)).astype(BF16)
        raw = lax.dot_general(window.astype(BF16), waveforms, BY_LANES, preferred_element_type=F32)
        power = lax.dot_general(high, ones, BY_LANES, preferred_element_type=F32)
        power += lax.dot_general(low, ones, BY_LANES, preferred_element_type=F32)
        ncc = (raw * lax.rsqrt(power + tmpl_len * 1e-05)).astype(BF16)
        for part in range(per_tile):
            d = tile * per_tile + part
            mine = ncc[LANES - (part + 1) * slab : LANES - part * slab]
            out_ref[places[d], MAXOFF:] = mine
            if d > 0:
                out_ref[places[d - 1], :MAXOFF] = mine[slab - MAXOFF :]


def stack_kernel(slab, row_count, moves_ref, weights_ref, parts_ref, out_ref, wide, moved):
    groups, rows, lanes = parts_ref.shape
    blocks = weights_ref.shape[0]
    tmpl_count = lanes // row_count
    pitch = groups + 1
    lane = lax.broadcasted_iota(jnp.int32, (slab, lanes), 1)
    wide[...] = parts_ref[...].astype(F32)
    moves = moves_ref[...]
    for src in range(groups):
        for b in range(blocks):
            moment = None
            for s in range(row_count):
                start = MAXOFF - moves[b, s * groups + src]
                piece = wide[src, pl.ds(start, slab), :]
                moment = piece if s == 0 else jnp.where(lane < s * tmpl_count, moment, piece)
            moved[b, pl.ds(src, slab, stride=pitch), :] = moment

    low_half = lax.broadcasted_iota(jnp.int32, (groups, lanes), 1) < tmpl_count
    times = 4
    for q in range(0, slab, times):
        best = None
        for b in range(blocks):
            columns = []
            for p in range(q, q + times, 2):
                even = moved[b, p * pitch : p * pitch + groups, :]
                odd = moved[b, (p + 1) * pitch : (p + 1) * pitch + groups, :]
                top = jnp.where(low_half, even, pltpu.roll(odd, tmpl_count, 1))
                bottom = jnp.where(low_half, pltpu.roll(even, tmpl_count, 1), odd)
                columns.append(jnp.concatenate([top, bottom], axis=0).astype(BF16))
            stacked = jnp.dot(
                weights_ref[b], jnp.concatenate(columns, axis=1), preferred_element_type=F32
            )
            peak = jnp.max(stacked, axis=0, keepdims=True)
            best = peak if b == 0 else jnp.maximum(best, peak)
        for p in range(times):
            row = slab - 1 - q - p
            out_ref[row : row + 1, :] = best[:, p * tmpl_count : (p + 1) * tmpl_count]


def in_hbm(array):
    return pltpu.with_memory_space_constraint(array, pltpu.HBM)


def on_device(traces, templates, station_of_slot, travel_offsets, stack_weights):
    groups = lax.axis_size("tm")
    row_count, tmpl_count, tmpl_len = templates.shape
    slab = (traces.shape[1] - tmpl_len + 1) // groups
    slots = station_of_slot.shape[0]
    blocks, nodes, unused = stack_weights.shape
    lanes = row_count * tmpl_count
    vmem = pl.BlockSpec(memory_space=pltpu.VMEM)
    hbm = pl.BlockSpec(memory_space=pltpu.HBM)
    sources = (traces, templates, station_of_slot[None], travel_offsets.T, jnp.swapaxes(stack_weights, 1, 2))

    parts, moves, weights = pl.pallas_call(
        lambda *refs: correlate_kernel(slab, *refs),
        out_shape=(
            jax.ShapeDtypeStruct((groups, slab + MAXOFF, lanes), BF16),
            jax.ShapeDtypeStruct((blocks, slots), jnp.int32),
            jax.ShapeDtypeStruct((blocks, nodes, slots), BF16),
        ),
        in_specs=[hbm] * len(sources),
        out_specs=(vmem, vmem, vmem),
        scratch_shapes=[
            *(pltpu.VMEM(a.shape, a.dtype) for a in sources),
            pltpu.VMEM((row_count, groups * slab + LANES + tmpl_len), F32),
            pltpu.SemaphoreType.DMA((len(sources),)),
        ],
        compiler_params=PARAMS,
        name="correlate",
    )(*(in_hbm(a) for a in sources))
    order = [device_at(place, groups) for place in range(groups)]
    received = lax.all_to_all(
        parts, "tm", split_axis=0, concat_axis=0, axis_index_groups=[order], tiled=True
    )
    peaks = pl.pallas_call(
        lambda *refs: stack_kernel(slab, row_count, *refs),
        out_shape=jax.ShapeDtypeStruct((slab, tmpl_count), F32),
        in_specs=[vmem, vmem, vmem],
        out_specs=vmem,
        scratch_shapes=[
            pltpu.VMEM((groups, slab + MAXOFF, lanes), F32),
            pltpu.VMEM((blocks, slab * (groups + 1), lanes), F32),
        ],
        compiler_params=PARAMS,
        name="stack",
    )(moves, weights, received)
    return peaks.T


def solution(mesh):
    return jax.shard_map(
        on_device,
        mesh=mesh,
        in_specs=(P(("parts", "tm"), None), P("tm", None, None), P(), P(), P()),
        out_specs=P("parts", "tm"),
        check_vma=False,
    )
```

```python
import math

import jax
import jax.numpy as jnp
from jax import lax
from jax.experimental import pallas as pl
from jax.experimental.pallas import tpu as pltpu
from jax.sharding import PartitionSpec as P

MAXOFF = 16
LANES = 128
OUTER = 16
STRIDE = 5
F32 = jnp.float32
BF16 = jnp.bfloat16
BY_LANES = (((1,), (1,)), ((), ()))
BY_ROWS = (((0,), (0,)), ((), ()))
PARAMS = pltpu.CompilerParams(vmem_limit_bytes=24 << 20)


def device_at(place, groups):
    outer = math.gcd(groups, OUTER)
    place = place * (STRIDE if math.gcd(groups, STRIDE) == 1 else 1) % groups
    device = (place % outer) * (groups // outer) + place // outer
    return device + 1 - 2 * (device % 2) if groups % 2 == 0 else device


def on_diagonal(blocks):
    zero = jnp.zeros_like(blocks[0])
    return jnp.concatenate(
        [
            jnp.concatenate([b if i == j else zero for j in range(len(blocks))], axis=1)
            for i, b in enumerate(blocks)
        ],
        axis=0,
    )


def slot_tables(row_count, stations_ref, offsets_ref, weights_ref, moves_ref, columns_ref):
    slots = stations_ref.shape[1]
    groups = slots // row_count
    first = lax.broadcasted_iota(jnp.int32, (slots, slots), 0)
    second = lax.broadcasted_iota(jnp.int32, (1, slots), 1)
    standing = (first == stations_ref[...]).astype(BF16)
    wanted = (first == device_at(second % groups, groups) * row_count + second // groups).astype(BF16)
    order = jnp.dot(standing, wanted, preferred_element_type=F32).astype(BF16)
    moves = jnp.dot(offsets_ref[...].astype(BF16), order, preferred_element_type=F32)
    moves_ref[...] = moves.astype(jnp.int32)
    for b in range(weights_ref.shape[0]):
        columns = lax.dot_general(weights_ref[b], order, BY_ROWS, preferred_element_type=F32)
        columns_ref[b] = columns.astype(BF16)


def correlate_kernel(slab, *refs):
    sources, (out_ref, moves_ref, columns_ref) = refs[:5], refs[5:8]
    held, samples, sems = refs[8:13], refs[13], refs[14]
    copies = [pltpu.make_async_copy(a, b, sems.at[i]) for i, (a, b) in enumerate(zip(sources, held))]
    for copy in copies:
        copy.start()
    traces_ref, templates_ref = held[:2]
    row_count, length = traces_ref.shape
    tmpl_len = templates_ref.shape[2]
    groups = out_ref.shape[0]
    per_tile = LANES // slab
    places = [0] * groups
    for place in range(groups):
        places[device_at(place, groups)] = place
    samples[...] = jnp.zeros_like(samples)
    out_ref[places[groups - 1], :MAXOFF] = jnp.zeros((MAXOFF, out_ref.shape[2]), BF16)
    ones = on_diagonal([jnp.ones(templates_ref.shape[1:], BF16)] * row_count)
    for copy in copies:
        copy.wait()
    samples[:, :length] = traces_ref[...].astype(F32)
    waveforms = on_diagonal([templates_ref[s] for s in range(row_count)])
    slot_tables(row_count, *held[2:], moves_ref, columns_ref)
    row = lax.broadcasted_iota(jnp.int32, (LANES, LANES), 0)
    lane = lax.broadcasted_iota(jnp.int32, (LANES, LANES), 1)

    def turned(s, tile):
        stretch = samples[s : s + 1, tile * LANES : (tile + 1) * LANES]
        return pltpu.roll(jnp.broadcast_to(stretch, (LANES, LANES)), 1, 1, stride=1, stride_axis=0)

    following = [turned(s, 0) for s in range(row_count)]
    for tile in range(groups * slab // LANES):
        present, following = following, [turned(s, tile + 1) for s in range(row_count)]
        windows = [jnp.where(lane <= row, a, b) for a, b in zip(present, following)]
        window = jnp.concatenate(windows, axis=1)
        square = window * window
        high = square.astype(BF16)
        low = (square - high.astype(F32)).astype(BF16)
        raw = lax.dot_general(window.astype(BF16), waveforms, BY_LANES, preferred_element_type=F32)
        power = lax.dot_general(high, ones, BY_LANES, preferred_element_type=F32)
        power += lax.dot_general(low, ones, BY_LANES, preferred_element_type=F32)
        ncc = (raw * lax.rsqrt(power + tmpl_len * 1e-05)).astype(BF16)
        for part in range(per_tile):
            d = tile * per_tile + part
            mine = ncc[LANES - (part + 1) * slab : LANES - part * slab]
            out_ref[places[d], MAXOFF:] = mine
            if d > 0:
                out_ref[places[d - 1], :MAXOFF] = mine[slab - MAXOFF :]


def stack_kernel(slab, row_count, moves_ref, weights_ref, parts_ref, out_ref, wide, moved):
    groups, rows, lanes = parts_ref.shape
    blocks = weights_ref.shape[0]
    tmpl_count = lanes // row_count
    pitch = groups + 1
    lane = lax.broadcasted_iota(jnp.int32, (slab, lanes), 1)
    wide[...] = parts_ref[...].astype(F32)
    moves = moves_ref[...]
    for src in range(groups):
        for b in range(blocks):
            moment = None
            for s in range(row_count):
                start = MAXOFF - moves[b, s * groups + src]
                piece = wide[src, pl.ds(start, slab), :]
                moment = piece if s == 0 else jnp.where(lane < s * tmpl_count, moment, piece)
            moved[b, pl.ds(src, slab, stride=pitch), :] = moment

    low_half = lax.broadcasted_iota(jnp.int32, (groups, lanes), 1) < tmpl_count
    times = 8
    for q in range(0, slab, times):
        best = None
        for b in range(blocks):
            columns = []
            for p in range(q, q + times, 2):
                even = moved[b, p * pitch : p * pitch + groups, :]
                odd = moved[b, (p + 1) * pitch : (p + 1) * pitch + groups, :]
                top = jnp.where(low_half, even, pltpu.roll(odd, tmpl_count, 1))
                bottom = jnp.where(low_half, pltpu.roll(even, tmpl_count, 1), odd)
                columns.append(jnp.concatenate([top, bottom], axis=0).astype(BF16))
            stacked = jnp.dot(
                weights_ref[b], jnp.concatenate(columns, axis=1), preferred_element_type=F32
            )
            peak = jnp.max(stacked, axis=0, keepdims=True)
            best = peak if b == 0 else jnp.maximum(best, peak)
        for p in range(times):
            row = slab - 1 - q - p
            out_ref[row : row + 1, :] = best[:, p * tmpl_count : (p + 1) * tmpl_count]


def in_hbm(array):
    return pltpu.with_memory_space_constraint(array, pltpu.HBM)


def on_device(traces, templates, station_of_slot, travel_offsets, stack_weights):
    groups = lax.axis_size("tm")
    row_count, tmpl_count, tmpl_len = templates.shape
    slab = (traces.shape[1] - tmpl_len + 1) // groups
    slots = station_of_slot.shape[0]
    blocks, nodes, unused = stack_weights.shape
    lanes = row_count * tmpl_count
    vmem = pl.BlockSpec(memory_space=pltpu.VMEM)
    hbm = pl.BlockSpec(memory_space=pltpu.HBM)
    sources = (traces, templates, station_of_slot[None], travel_offsets.T, jnp.swapaxes(stack_weights, 1, 2))

    parts, moves, weights = pl.pallas_call(
        lambda *refs: correlate_kernel(slab, *refs),
        out_shape=(
            jax.ShapeDtypeStruct((groups, slab + MAXOFF, lanes), BF16),
            jax.ShapeDtypeStruct((blocks, slots), jnp.int32),
            jax.ShapeDtypeStruct((blocks, nodes, slots), BF16),
        ),
        in_specs=[hbm] * len(sources),
        out_specs=(vmem, vmem, vmem),
        scratch_shapes=[
            *(pltpu.VMEM(a.shape, a.dtype) for a in sources),
            pltpu.VMEM((row_count, groups * slab + LANES + tmpl_len), F32),
            pltpu.SemaphoreType.DMA((len(sources),)),
        ],
        compiler_params=PARAMS,
        name="correlate",
    )(*(in_hbm(a) for a in sources))
    order = [device_at(place, groups) for place in range(groups)]
    received = lax.all_to_all(
        parts, "tm", split_axis=0, concat_axis=0, axis_index_groups=[order], tiled=True
    )
    peaks = pl.pallas_call(
        lambda *refs: stack_kernel(slab, row_count, *refs),
        out_shape=jax.ShapeDtypeStruct((slab, tmpl_count), F32),
        in_specs=[vmem, vmem, vmem],
        out_specs=vmem,
        scratch_shapes=[
            pltpu.VMEM((groups, slab + MAXOFF, lanes), F32),
            pltpu.VMEM((blocks, slab * (groups + 1), lanes), F32),
        ],
        compiler_params=PARAMS,
        name="stack",
    )(moves, weights, received)
    return peaks.T


def solution(mesh):
    return jax.shard_map(
        on_device,
        mesh=mesh,
        in_specs=(P(("parts", "tm"), None), P("tm", None, None), P(), P(), P()),
        out_specs=P("parts", "tm"),
        check_vma=False,
    )
```
